32 devices in a mesh: grp: 2 (over x), lon: 8 (over z, y), lat: 2 (over core).
Axes of the slice: x: 2, y: 2, z: 4, core: 2. Of those that a mesh axis runs over, the one named last changes fastest.
Arguments:
- right_side: float32 [8, 10, 64, 1024], P('grp', None, 'lat', 'lon'), parts along dimension 0, may hold values from -6 to 6
- kappa_sq: float32 [10, 64, 1024], P(None, 'lat', 'lon'), may hold values from 0.02 to 0.7
- flux_x: float32 [10, 64, 1024], P(None, 'lat', 'lon'), may hold values from 0.07 to 0.7
- flux_y: float32 [10, 64, 1024], P(None, 'lat', 'lon'), may hold values from 0.07 to 0.7
- flux_z: float32 [10, 64, 1024], P(None, 'lat', 'lon'), may hold values from 0.035 to 0.35
- wet_mask: int32 [10, 64, 1024], P(None, 'lat', 'lon'), may hold values from 0 to 1
- obs_cells: int32 [2, 8, 2048], P('lat', 'lon'), may hold values from 0 to 40959
- obs_weight: float32 [2, 8, 2048], P('lat', 'lon'), may hold values from 0.2 to 8
- obs_data: float32 [8, 2, 8, 2048], P('grp', 'lat', 'lon'), parts along dimension 0, may hold values from -6 to 6
Outputs:
- sample_field: float32 [8, 10, 64, 1024], P('grp', None, 'lat', 'lon'), parts along dimension 0
The draws below stay inside these ranges and needn't reach their ends.
There are 2 independent parts, one for each index of `grp`. The reference program is written for one: setup_inputs(seed, part) draws one part's arguments, and reference() takes and returns one part's arrays. A program takes and returns all parts, laid end to end along the dimension named above; an argument that names none is the same for every part. Nothing has to cross between parts.
All inputs are finite; a program needn't handle non-finite values.
Results may differ from the reference program's by a relative error of at most 0.0001.
Values sent between devices are 32-bit elements; how exact they have to be, the bound alone decides.
A program may use at most 128 MiB of HBM per device.

```python
import math
import jax
import jax.numpy as jnp

CX = 128
CY = 32
NZ = 10
K = 4
OBS_DEV = 2048
ITERS = 2
NX = 1024
NY = 64
N_LON = 8
N_LAT = 2


def draw_wet_mask(key, part):
    key = jax.random.fold_in(key, 7)
    floor_key = jax.random.fold_in(key, 1)
    shore_key = jax.random.fold_in(key, 2)
    brick_cols = CX // 2
    floors = jax.random.randint(floor_key, (NY // CY, NX // brick_cols), -3, NZ + 1)
    floors = jnp.repeat(jnp.repeat(floors, CY, axis=0), brick_cols, axis=1)
    jitter = jax.random.randint(shore_key, (NZ, NY, NX), -1, 2)
    levels = jnp.arange(NZ, dtype=jnp.int32)[:, None, None]
    wet = jnp.logical_and(floors[None] > 0, levels < floors[None] + jitter)
    return wet.astype(jnp.int32)


def place_ends(result, key, least, high):
    extent = result.shape
    index_at = [jax.random.randint(jax.random.fold_in(key, axis), (), 0, extent[axis]) for axis in range(len(extent))]
    result = result.at[tuple(index_at)].set(least)
    longest = extent.index(max(extent))
    index_at[longest] = (index_at[longest] + 1) % extent[longest]
    return result.at[tuple(index_at)].set(high)


def shard_levels(rng, shape, cuts, least, high):
    def one(axis_at, blocks):
        steps = jax.random.uniform(jax.random.fold_in(jax.random.fold_in(rng, 6), axis_at), (blocks,), jnp.float32, least / len(cuts), high / len(cuts))
        return jnp.repeat(jnp.exp(steps), shape[axis_at] // blocks).reshape((-1,) + (1,) * (len(shape) - axis_at - 1))

    gain = one(*cuts[0])
    for cut in cuts[1:]:
        gain = gain * one(*cut)
    return gain


def centred(rng, extent, spread, most, shards=(), held_as=jnp.bfloat16):
    level = shard_levels(rng, extent, shards, -0.22, 0.18) if shards else 1.0
    result = jax.random.normal(rng, extent, jnp.float32) * spread * level
    return jnp.minimum(jnp.maximum(result, -most), most).astype(held_as)


def setup_inputs(seed: int = 0, part: int = 0) -> dict:
    key_of = jax.random.split(jax.random.key(seed), 10)
    part_keys = jax.random.split(jax.random.fold_in(key_of[9], part), 10)
    return {
        "right_side": centred(part_keys[0], (K, NZ, NY, NX), 1.0, 6.0, ((2, 2), (3, 8)), jnp.float32),
        "kappa_sq": jnp.clip(jnp.exp(math.log(0.7) - 3.5553481 * jax.random.uniform(key_of[1], (NZ, NY, NX), jnp.float32) ** shard_levels(key_of[1], (NZ, NY, NX), ((1, 2), (2, 8)), -0.2, 0.2)), 0.02, 0.7),
        "flux_x": jnp.clip(jnp.exp(math.log(0.7) - 2.3025851 * jax.random.uniform(key_of[2], (NZ, NY, NX), jnp.float32) ** shard_levels(key_of[2], (NZ, NY, NX), ((1, 2), (2, 8)), -0.2, 0.2)), 0.07, 0.7),
        "flux_y": jnp.clip(jnp.exp(math.log(0.7) - 2.3025851 * jax.random.uniform(key_of[3], (NZ, NY, NX), jnp.float32) ** shard_levels(key_of[3], (NZ, NY, NX), ((1, 2), (2, 8)), -0.2, 0.2)), 0.07, 0.7),
        "flux_z": jnp.clip(jnp.exp(math.log(0.35) - 2.3025851 * jax.random.uniform(key_of[4], (NZ, NY, NX), jnp.float32) ** shard_levels(key_of[4], (NZ, NY, NX), ((1, 2), (2, 8)), -0.2, 0.2)), 0.035, 0.35),
        "wet_mask": draw_wet_mask(jax.random.fold_in(key_of[9], 71), part),
        "obs_cells": place_ends(jax.random.randint(key_of[6], (N_LAT, N_LON, OBS_DEV), 0, NZ * CY * CX), jax.random.fold_in(key_of[6], 1), 0, (NZ * CY * CX) - 1).astype(jnp.int32),
        "obs_weight": jnp.clip(jnp.exp(math.log(8.0) - 3.6888794 * jax.random.uniform(key_of[7], (N_LAT, N_LON, OBS_DEV), jnp.float32) ** shard_levels(key_of[7], (N_LAT, N_LON, OBS_DEV), ((0, 2), (1, 8)), -0.2, 0.2)), 0.2, 8.0),
        "obs_data": centred(part_keys[8], (K, N_LAT, N_LON, OBS_DEV), 1.0, 6.0, ((1, 2), (2, 8)), jnp.float32),
    }


def pad_grid(field, width):
    field = jnp.concatenate([field[..., -width:], field, field[..., :width]], axis=-1)
    config = [(0, 0)] * (field.ndim - 2) + [(width, width), (0, 0)]
    return jnp.pad(field, config)


def center(field):
    return field[..., 1:-1, 1:-1]


def masked_pass(padded, coefs):
    kappa, hx_face, hy_face, hz_face, maskf = coefs
    masked = maskf * padded
    inner = center(masked)
    zconfig = [(0, 0)] * (inner.ndim - 3) + [(1, 1), (0, 0), (0, 0)]
    deeper = jnp.pad(inner, zconfig)
    hz_here = center(hz_face)
    hz_above = jnp.pad(hz_here, ((1, 0), (0, 0), (0, 0)))[:-1]
    total = center(kappa) * inner
    total = total + center(hx_face) * (inner - masked[..., 1:-1, 2:])
    total = total + hx_face[:, 1:-1, :-2] * (inner - masked[..., 1:-1, :-2])
    total = total + center(hy_face) * (inner - masked[..., 2:, 1:-1])
    total = total + hy_face[:, :-2, 1:-1] * (inner - masked[..., :-2, 1:-1])
    total = total + hz_here * (inner - deeper[..., 2:, :, :])
    total = total + hz_above * (inner - deeper[..., :-2, :, :])
    mask_inner = center(maskf)
    return mask_inner * total + (1.0 - mask_inner) * center(padded)


def precond_diag(coefs, obs_prec):
    kappa, hx_face, hy_face, hz_face, maskf = coefs
    hz_here = center(hz_face)
    hz_above = jnp.pad(hz_here, ((1, 0), (0, 0), (0, 0)))[:-1]
    diag_l = center(kappa) + center(hx_face) + hx_face[:, 1:-1, :-2] + center(hy_face) + hy_face[:, :-2, 1:-1] + hz_here + hz_above
    mask_inner = center(maskf)
    scaled = mask_inner * diag_l + (1.0 - mask_inner)
    return 1.0 / (scaled * scaled + obs_prec)


def inner_sums(left, right):
    return jnp.sum(left * right, axis=(1, 2, 3))


def reference(right_side, kappa_sq, flux_x, flux_y, flux_z, wet_mask, obs_cells, obs_weight, obs_data):
    maskf = wet_mask.astype(jnp.float32)
    coefs = tuple(pad_grid(a, 1) for a in (kappa_sq, flux_x, flux_y, flux_z, maskf))
    lat_ids = jnp.arange(N_LAT, dtype=jnp.int32)[:, None, None]
    lon_ids = jnp.arange(N_LON, dtype=jnp.int32)[None, :, None]
    level = obs_cells // (CY * CX)
    row = lat_ids * CY + (obs_cells // CX) % CY
    col = lon_ids * CX + obs_cells % CX
    flat = ((level * NY + row) * NX + col).reshape(-1)
    cells = NZ * NY * NX
    obs_prec = jnp.zeros((cells,), jnp.float32).at[flat].add(obs_weight.reshape(-1)).reshape(NZ, NY, NX)
    valued = (obs_weight[None] * obs_data).reshape(K, -1)
    shift = jnp.zeros((K, cells), jnp.float32).at[:, flat].add(valued).reshape(K, NZ, NY, NX)
    rhs = right_side + shift
    prec = precond_diag(coefs, obs_prec)

    def apply_op(field):
        once = masked_pass(pad_grid(field, 1), coefs)
        twice = masked_pass(pad_grid(once, 1), coefs)
        return twice + obs_prec * field

    solution = jnp.zeros_like(rhs)
    resid = rhs
    zvec = prec * resid
    direction = zvec
    gamma = inner_sums(resid, zvec)
    for step in range(ITERS):
        image = apply_op(direction)
        alpha = gamma / inner_sums(direction, image)
        solution = solution + alpha[:, None, None, None] * direction
        resid = resid - alpha[:, None, None, None] * image
        if step + 1 < ITERS:
            zvec = prec * resid
            gamma_new = inner_sums(resid, zvec)
            direction = zvec + (gamma_new / gamma)[:, None, None, None] * direction
            gamma = gamma_new
    return solution
```

```python
import functools

import jax
import jax.numpy as jnp
from jax import lax
from jax.experimental import pallas as pl
from jax.experimental.pallas import tpu as pltpu
from jax.sharding import PartitionSpec as P

MESH = pl.DeviceIdType.MESH
PAD = 8
F32 = jnp.float32


def kernel(
    n_lon, rs_ref, ka_ref, fx_ref, fy_ref, fz_ref, wm_ref, oc_ref, ow_ref, od_ref, out_ref,
    row_hot, bs, ops, prec, dg, cx, cxl, cy, cyu, cz, fa, fb, ww,
    col_send, col_recv, row_send, row_recv, part, slots, tot,
    send_sem, recv_sem, red_send, red_recv,
):
    samples, levels, rows, cols = rs_ref.shape
    blocks = rows // 8
    high = rows + 2 * PAD
    per_level = samples * blocks
    per_vreg = cols // per_level
    grp, lon, lat = lax.axis_index("grp"), lax.axis_index("lon"), lax.axis_index("lat")
    right = lax.rem(lon + 1, n_lon)
    left = lax.rem(lon + n_lon - 1, n_lon)
    group = 2 * n_lon
    me = lon * 2 + lat

    def peer(step):
        other = lax.rem(me + step, group)
        return (grp, other // 2, lax.rem(other, 2))

    barrier = pltpu.get_barrier_semaphore()
    for step in range(1, group):
        pl.semaphore_signal(barrier, inc=1, device_id=peer(step), device_id_type=MESH)

    is_low = lat == 0
    lane1 = lax.broadcasted_iota(jnp.int32, (8, cols), 1)
    lane32 = lax.broadcasted_iota(jnp.int32, (rows, cols), 1)
    row32 = lax.broadcasted_iota(jnp.int32, (rows, cols), 0)
    first_lane, last_lane = lane32 == 0, lane32 == cols - 1
    edge = jnp.where(is_low, rows - 1, 0)

    def exchange(slot):
        copies = []
        for side, target in ((0, (grp, right, lat)), (1, (grp, left, lat))):
            copies.append(pltpu.make_async_remote_copy(
                src_ref=col_send.at[slot, side], dst_ref=col_recv.at[slot, side],
                send_sem=send_sem.at[slot, side], recv_sem=recv_sem.at[slot, side],
                device_id=target, device_id_type=MESH))
        copies.append(pltpu.make_async_remote_copy(
            src_ref=row_send.at[slot], dst_ref=row_recv.at[slot],
            send_sem=send_sem.at[slot, 2], recv_sem=recv_sem.at[slot, 2],
            device_id=(grp, lon, 1 - lat), device_id_type=MESH))
        for copy in copies:
            copy.start()
        return copies

    def reduce_start(which):
        copies = []
        for step in range(1, group):
            copies.append(pltpu.make_async_remote_copy(
                src_ref=part.at[which], dst_ref=slots.at[which, step - 1],
                send_sem=red_send.at[which, step - 1], recv_sem=red_recv.at[which, step - 1],
                device_id=peer(step), device_id_type=MESH))
        for copy in copies:
            copy.start()
        return copies

    def reduce_finish(which, copies):
        total = part[which]
        for step, copy in enumerate(copies):
            copy.wait()
            total = total + slots[which, step]
        tot[which] = jnp.broadcast_to(jnp.sum(total, axis=1, keepdims=True), total.shape)

    to_right = jnp.zeros((8, cols), F32)
    to_left = jnp.zeros((8, cols), F32)
    for z in range(levels):
        for y in range(blocks):
            at = z * blocks + y
            here = pl.ds(y * 8, 8)
            flux = fx_ref[z, here, :]
            mask = wm_ref[z, here, :].astype(F32)
            to_right = jnp.where(lane1 == at, flux[:, cols - 1:cols], to_right)
            to_right = jnp.where(lane1 == at + cols // 2, mask[:, cols - 1:cols], to_right)
            to_left = jnp.where(lane1 == at, mask[:, 0:1], to_left)
    col_send[0, 0, 0] = to_right
    col_send[0, 1, 0] = to_left
    col_send[0, 0, 1] = jnp.zeros((8, cols), F32)
    col_send[0, 1, 1] = jnp.zeros((8, cols), F32)
    row_send[0] = jnp.zeros(row_send.shape[1:], F32)
    for z in range(levels):
        row_send[0, z:z + 1, :] = jnp.where(is_low, fy_ref[z, rows - 1:rows, :], fy_ref[z, 0:1, :])
        row_send[0, levels + z:levels + z + 1, :] = jnp.where(
            is_low, wm_ref[z, rows - 1:rows, :], wm_ref[z, 0:1, :]).astype(F32)

    pl.semaphore_wait(barrier, group - 1)
    copies = exchange(0)

    count = oc_ref.shape[-1]
    cells = oc_ref[0]
    flat_rows = levels * rows
    hot = lax.broadcasted_iota(jnp.int32, (flat_rows, count), 0) == cells // cols
    row_hot[...] = jnp.where(hot, 1.0, 0.0).astype(jnp.bfloat16)
    lane_hot = lax.broadcasted_iota(jnp.int32, (cols, count), 0) == lax.rem(cells, cols)
    weight = ow_ref[0]

    def scatter(value):
        top = value.astype(jnp.bfloat16).astype(F32)
        low = value - top
        both = jnp.concatenate(
            [jnp.where(lane_hot, top, 0.0), jnp.where(lane_hot, low, 0.0)], axis=0
        ).astype(jnp.bfloat16)
        got = lax.dot_general(
            row_hot[...], both, (((1,), (1,)), ((), ())), preferred_element_type=F32)
        return (got[:, :cols] + got[:, cols:]).reshape(levels, rows, cols)

    ops[...] = scatter(weight)
    for k in range(samples):
        bs[k] = rs_ref[k] + scatter(weight * od_ref[k, 0])

    for copy in copies:
        copy.wait()

    from_left, from_right = col_recv[0, 0, 0], col_recv[0, 1, 0]

    def column(packed, at):
        return jnp.concatenate(
            [jnp.broadcast_to(packed[:, at + y:at + y + 1], (8, cols)) for y in range(blocks)],
            axis=0)

    above = jnp.zeros((rows, cols), F32)
    for z in range(levels):
        mask = wm_ref[z].astype(F32)
        flux_x, flux_y, flux_z = fx_ref[z], fy_ref[z], fz_ref[z]
        at = z * blocks
        fx_left = jnp.where(first_lane, column(from_left, at), pltpu.roll(flux_x, 1, 1))
        m_left = jnp.where(first_lane, column(from_left, at + cols // 2), pltpu.roll(mask, 1, 1))
        m_right = jnp.where(last_lane, column(from_right, at), pltpu.roll(mask, cols - 1, 1))
        halo_fy = row_recv[0, z:z + 1, :]
        halo_m = row_recv[0, levels + z:levels + z + 1, :]
        fy_up = jnp.where(row32 == 0, jnp.where(is_low, 0.0, halo_fy), pltpu.roll(flux_y, 1, 0))
        m_up = jnp.where(row32 == 0, jnp.where(is_low, 0.0, halo_m), pltpu.roll(mask, 1, 0))
        m_down = jnp.where(
            row32 == rows - 1, jnp.where(is_low, halo_m, 0.0), pltpu.roll(mask, rows - 1, 0))
        diag = ka_ref[z] + flux_x + fx_left + flux_y + fy_up + flux_z + above
        scaled = mask * diag + (1.0 - mask)
        dg[z] = scaled
        prec[z] = 1.0 / (scaled * scaled + ops[z])
        cx[z] = flux_x * mask * m_right
        cxl[z] = fx_left * mask * m_left
        cy[z] = flux_y * mask * m_down
        cyu[z] = fy_up * mask * m_up
        if z + 1 < levels:
            cz[z] = flux_z * mask * wm_ref[z + 1].astype(F32)
        above = flux_z

    def base(k, z):
        return (k * levels + z) * high

    group_lane = lax.broadcasted_iota(jnp.int32, (per_level, 8, cols), 2) - lax.broadcasted_iota(
        jnp.int32, (per_level, 8, cols), 0)

    class Packer:
        def __init__(self):
            self.acc = [[jnp.zeros((8, cols), F32)] * 2 for _ in range(2)]

        def add(self, z, values):
            half, at = z // per_vreg, (z % per_vreg) * per_level
            tiles = jnp.stack(values).reshape(per_level, 8, cols)
            here = group_lane == at
            for side, lane in ((0, cols - 1), (1, 0)):
                edge_col = jnp.broadcast_to(tiles[:, :, lane:lane + 1], tiles.shape)
                self.acc[side][half] = self.acc[side][half] + jnp.sum(
                    jnp.where(here, edge_col, 0.0), axis=0)

        def send(self, slot, field):
            for side in range(2):
                for half in range(2):
                    col_send[slot, side, half] = self.acc[side][half]
            low = field[pl.ds(PAD, samples * levels, stride=high), :]
            top = field[pl.ds(PAD + rows - 1, samples * levels, stride=high), :]
            row_send[slot] = jnp.where(is_low, top, low)
            return exchange(slot)

    def put_rows(slot, field):
        got = row_recv[slot]
        field[pl.ds(PAD - 1, samples * levels, stride=high), :] = jnp.where(is_low, 0.0, got)
        field[pl.ds(PAD + rows, samples * levels, stride=high), :] = jnp.where(is_low, got, 0.0)

    def apply(slot, field, k, z, packs):
        at = base(k, z) + PAD
        here = field[pl.ds(at, rows), :]
        up = field[pl.ds(at - 1, rows), :]
        down = field[pl.ds(at + 1, rows), :]
        half, lane = z // per_vreg, (z % per_vreg) * per_level + k * blocks
        west = jnp.where(first_lane, column(packs[0][half], lane), pltpu.roll(here, 1, 1))
        east = jnp.where(last_lane, column(packs[1][half], lane), pltpu.roll(here, cols - 1, 1))
        total = dg[z] * here - cx[z] * east - cxl[z] * west - cy[z] * down - cyu[z] * up
        if z > 0:
            total = total - cz[z - 1] * field[pl.ds(at - high, rows), :]
        if z + 1 < levels:
            total = total - cz[z] * field[pl.ds(at + high, rows), :]
        return here, total

    def received(slot):
        return [[col_recv[slot, side, half] for half in range(2)] for side in range(2)]

    def fold(value):
        return jnp.sum(value.reshape(blocks, 8, cols), axis=0)

    def store_parts(which, sums):
        for at, value in enumerate(sums):
            part[which, at:at + 1, :] = jnp.sum(value, axis=0, keepdims=True)

    zero = jnp.zeros((8, cols), F32)

    packer = Packer()
    sums = [zero] * (2 * samples)
    for z in range(levels):
        values = []
        for k in range(samples):
            b = bs[k, z]
            p = prec[z] * b
            fa[pl.ds(base(k, z) + PAD, rows), :] = p
            sums[k] = sums[k] + fold(p * b)
            values.append(p)
        packer.add(z, values)
    copies = packer.send(1, fa)
    for copy in copies:
        copy.wait()
    put_rows(1, fa)

    packs = received(1)
    packer = Packer()
    for z in range(levels):
        values = []
        for k in range(samples):
            p, u = apply(1, fa, k, z, packs)
            fb[pl.ds(base(k, z) + PAD, rows), :] = u
            sums[samples + k] = sums[samples + k] + fold(u * u + ops[z] * p * p)
            values.append(u)
        packer.add(z, values)
    store_parts(0, sums)
    copies = packer.send(2, fb)
    red = reduce_start(0)
    for copy in copies:
        copy.wait()
    put_rows(2, fb)

    packs = received(2)
    packer = Packer()
    for z in range(levels):
        values = []
        for k in range(samples):
            _, q = apply(2, fb, k, z, packs)
            q = q + ops[z] * fa[pl.ds(base(k, z) + PAD, rows), :]
            w = prec[z] * q
            out_ref[k, z] = q
            ww[pl.ds(base(k, z) + PAD, rows), :] = w
            values.append(w)
        packer.add(z, values)
    copies = packer.send(3, ww)
    reduce_finish(0, red)
    gamma = [tot[0, k:k + 1, :] for k in range(samples)]
    den = [tot[0, samples + k:samples + k + 1, :] for k in range(samples)]
    alpha = [g / d for g, d in zip(gamma, den)]
    sums = [zero] * (2 * samples)
    for z in range(levels):
        for k in range(samples):
            r = bs[k, z] - alpha[k] * out_ref[k, z]
            zv = prec[z] * r
            sums[k] = sums[k] + fold(zv * r)
            fb[pl.ds(base(k, z) + PAD, rows), :] = zv
    for copy in copies:
        copy.wait()

    got = row_recv[3]
    span = samples * levels
    sample_of = lax.broadcasted_iota(jnp.int32, (span, cols), 0) // levels
    alpha_rows = jnp.zeros((span, cols), F32)
    for k in range(samples):
        alpha_rows = jnp.where(sample_of == k, alpha[k], alpha_rows)
    halo = row_recv[1] - alpha_rows * got
    fb[pl.ds(PAD - 1, span, stride=high), :] = jnp.where(is_low, 0.0, halo)
    fb[pl.ds(PAD + rows, span, stride=high), :] = jnp.where(is_low, halo, 0.0)
    lane_sample = lax.rem(lane1, per_level) // blocks
    alpha_lanes = jnp.zeros((8, cols), F32)
    for k in range(samples):
        alpha_lanes = jnp.where(lane_sample == k, alpha[k], alpha_lanes)
    packs = [
        [a - alpha_lanes * b for a, b in zip(first, second)]
        for first, second in zip(received(1), received(3))
    ]
    for z in range(levels):
        for k in range(samples):
            zv, u = apply(3, fb, k, z, packs)
            sums[samples + k] = sums[samples + k] + fold(u * u + ops[z] * zv * zv)
    store_parts(1, sums)
    red = reduce_start(1)
    reduce_finish(1, red)
    for k in range(samples):
        new = tot[1, k:k + 1, :]
        beta = new / gamma[k]
        step = new / (tot[1, samples + k:samples + k + 1, :] - beta * beta * den[k])
        p_scale = alpha[k] + step * beta
        for z in range(levels):
            at = pl.ds(base(k, z) + PAD, rows)
            out_ref[k, z] = p_scale * fa[at, :] + step * fb[at, :]


def per_device(n_lon, rs, ka, fx, fy, fz, wm, oc, ow, od):
    samples, levels, rows, cols = rs.shape
    count = oc.shape[-1]
    cell = (levels, rows, cols)
    high = rows + 2 * PAD
    field = pltpu.VMEM((samples * levels * high, cols), F32)
    group = 2 * n_lon
    coef = pltpu.VMEM(cell, F32)
    vmem = pl.BlockSpec(memory_space=pltpu.VMEM)
    return pl.pallas_call(
        functools.partial(kernel, n_lon),
        out_shape=jax.ShapeDtypeStruct(rs.shape, F32),
        in_specs=[vmem] * 9,
        out_specs=vmem,
        scratch_shapes=[
            pltpu.VMEM((levels * rows, count), jnp.bfloat16),
            pltpu.VMEM(rs.shape, F32),
            coef, coef, coef, coef, coef, coef, coef, coef,
            field, field, field,
            pltpu.VMEM((4, 2, 2, 8, cols), F32),
            pltpu.VMEM((4, 2, 2, 8, cols), F32),
            pltpu.VMEM((4, samples * levels, cols), F32),
            pltpu.VMEM((4, samples * levels, cols), F32),
            pltpu.VMEM((2, 2 * samples, cols), F32),
            pltpu.VMEM((2, group - 1, 2 * samples, cols), F32),
            pltpu.VMEM((2, 2 * samples, cols), F32),
            pltpu.SemaphoreType.DMA((4, 3)),
            pltpu.SemaphoreType.DMA((4, 3)),
            pltpu.SemaphoreType.DMA((2, group - 1)),
            pltpu.SemaphoreType.DMA((2, group - 1)),
        ],
        compiler_params=pltpu.CompilerParams(
            collective_id=0, has_side_effects=True, vmem_limit_bytes=40 * 1024 * 1024),
        cost_estimate=pl.CostEstimate(
            flops=4 * 10**9, bytes_accessed=3 * 10**6, transcendentals=0),
    )(rs, ka, fx, fy, fz, wm, oc, ow, od)


def solution(mesh):
    assert mesh.shape["lat"] == 2
    return jax.shard_map(
        functools.partial(per_device, mesh.shape["lon"]),
        mesh=mesh,
        in_specs=(
            P("grp", None, "lat", "lon"),
            P(None, "lat", "lon"),
            P(None, "lat", "lon"),
            P(None, "lat", "lon"),
            P(None, "lat", "lon"),
            P(None, "lat", "lon"),
            P("lat", "lon", None),
            P("lat", "lon", None),
            P("grp", "lat", "lon", None),
        ),
        out_specs=P("grp", None, "lat", "lon"),
        check_vma=False,
    )
```

```python
import functools

import jax
import jax.numpy as jnp
from jax import lax
from jax.experimental import pallas as pl
from jax.experimental.pallas import tpu as pltpu
from jax.sharding import PartitionSpec as P

MESH = pl.DeviceIdType.MESH
PAD = 8
F32 = jnp.float32


def kernel(
    n_lon, rs_in, ka_in, fx_in, fy_in, fz_in, wm_in, oc_in, ow_in, od_in, out_ref,
    rs_ref, ka_ref, fx_ref, fy_ref, fz_ref, wm_ref, oc_ref, ow_ref, od_ref,
    row_hot, bs, ops, prec, dg, cx, cxl, cy, cyu, cz, fa, fb, ww,
    col_send, col_recv, row_send, row_recv, part, slots, tot,
    send_sem, recv_sem, red_send, red_recv, load_sem,
):
    samples, levels, rows, cols = rs_ref.shape
    blocks = rows // 8
    high = rows + 2 * PAD
    per_level = samples * blocks
    per_vreg = cols // per_level
    grp, lon, lat = lax.axis_index("grp"), lax.axis_index("lon"), lax.axis_index("lat")
    right = lax.rem(lon + 1, n_lon)
    left = lax.rem(lon + n_lon - 1, n_lon)
    group = 2 * n_lon
    me = lon * 2 + lat

    def peer(step):
        other = lax.rem(me + step, group)
        return (grp, other // 2, lax.rem(other, 2))

    pairs = (
        (wm_in, wm_ref), (fx_in, fx_ref), (fy_in, fy_ref), (oc_in, oc_ref), (ow_in, ow_ref),
        (od_in, od_ref), (rs_in, rs_ref), (ka_in, ka_ref), (fz_in, fz_ref))
    loads = [
        pltpu.make_async_copy(source, here, load_sem.at[at])
        for at, (source, here) in enumerate(pairs)]
    for load in loads:
        load.start()
    barrier = pltpu.get_barrier_semaphore()
    for step in range(1, group):
        pl.semaphore_signal(barrier, inc=1, device_id=peer(step), device_id_type=MESH)

    is_low = lat == 0
    lane1 = lax.broadcasted_iota(jnp.int32, (8, cols), 1)
    lane32 = lax.broadcasted_iota(jnp.int32, (rows, cols), 1)
    row32 = lax.broadcasted_iota(jnp.int32, (rows, cols), 0)
    first_lane, last_lane = lane32 == 0, lane32 == cols - 1

    def exchange(slot):
        copies = []
        for side, target in ((0, (grp, right, lat)), (1, (grp, left, lat))):
            copies.append(pltpu.make_async_remote_copy(
                src_ref=col_send.at[slot, side], dst_ref=col_recv.at[slot, side],
                send_sem=send_sem.at[slot, side], recv_sem=recv_sem.at[slot, side],
                device_id=target, device_id_type=MESH))
        copies.append(pltpu.make_async_remote_copy(
            src_ref=row_send.at[slot], dst_ref=row_recv.at[slot],
            send_sem=send_sem.at[slot, 2], recv_sem=recv_sem.at[slot, 2],
            device_id=(grp, lon, 1 - lat), device_id_type=MESH))
        for copy in copies:
            copy.start()
        return copies

    def reduce_start(which):
        copies = []
        for step in range(1, group):
            copies.append(pltpu.make_async_remote_copy(
                src_ref=part.at[which], dst_ref=slots.at[which, step - 1],
                send_sem=red_send.at[which, step - 1], recv_sem=red_recv.at[which, step - 1],
                device_id=peer(step), device_id_type=MESH))
        for copy in copies:
            copy.start()
        return copies

    def reduce_finish(which, copies):
        total = part[which]
        for step, copy in enumerate(copies):
            copy.wait()
            total = total + slots[which, step]
        tot[which] = jnp.broadcast_to(jnp.sum(total, axis=1, keepdims=True), total.shape)

    for load in loads[:3]:
        load.wait()

    to_right = jnp.zeros((8, cols), F32)
    to_left = jnp.zeros((8, cols), F32)
    for z in range(levels):
        for y in range(blocks):
            at = z * blocks + y
            here = pl.ds(y * 8, 8)
            flux = fx_ref[z, here, :]
            mask = wm_ref[z, here, :].astype(F32)
            to_right = jnp.where(lane1 == at, flux[:, cols - 1:cols], to_right)
            to_right = jnp.where(lane1 == at + cols // 2, mask[:, cols - 1:cols], to_right)
            to_left = jnp.where(lane1 == at, mask[:, 0:1], to_left)
    col_send[0, 0, 0] = to_right
    col_send[0, 1, 0] = to_left
    col_send[0, 0, 1] = jnp.zeros((8, cols), F32)
    col_send[0, 1, 1] = jnp.zeros((8, cols), F32)
    row_send[0] = jnp.zeros(row_send.shape[1:], F32)
    for z in range(levels):
        row_send[0, z:z + 1, :] = jnp.where(is_low, fy_ref[z, rows - 1:rows, :], fy_ref[z, 0:1, :])
        row_send[0, levels + z:levels + z + 1, :] = jnp.where(
            is_low, wm_ref[z, rows - 1:rows, :], wm_ref[z, 0:1, :]).astype(F32)

    pl.semaphore_wait(barrier, group - 1)
    copies = exchange(0)

    for load in loads[3:]:
        load.wait()

    count = oc_ref.shape[-1]
    cells = oc_ref[0]
    flat_rows = levels * rows
    hot = lax.broadcasted_iota(jnp.int32, (flat_rows, count), 0) == cells // cols
    row_hot[...] = jnp.where(hot, 1.0, 0.0).astype(jnp.bfloat16)
    lane_hot = lax.broadcasted_iota(jnp.int32, (cols, count), 0) == lax.rem(cells, cols)
    weight = ow_ref[0]

    def scatter(value):
        top = value.astype(jnp.bfloat16).astype(F32)
        low = value - top
        both = jnp.concatenate(
            [jnp.where(lane_hot, top, 0.0), jnp.where(lane_hot, low, 0.0)], axis=0
        ).astype(jnp.bfloat16)
        got = lax.dot_general(
            row_hot[...], both, (((1,), (1,)), ((), ())), preferred_element_type=F32)
        return (got[:, :cols] + got[:, cols:]).reshape(levels, rows, cols)

    ops[...] = scatter(weight)
    for k in range(samples):
        bs[k] = rs_ref[k] + scatter(weight * od_ref[k, 0])

    for copy in copies:
        copy.wait()

    from_left, from_right = col_recv[0, 0, 0], col_recv[0, 1, 0]

    def column(packed, at):
        return jnp.concatenate(
            [jnp.broadcast_to(packed[:, at + y:at + y + 1], (8, cols)) for y in range(blocks)],
            axis=0)

    above = jnp.zeros((rows, cols), F32)
    for z in range(levels):
        mask = wm_ref[z].astype(F32)
        flux_x, flux_y, flux_z = fx_ref[z], fy_ref[z], fz_ref[z]
        at = z * blocks
        fx_left = jnp.where(first_lane, column(from_left, at), pltpu.roll(flux_x, 1, 1))
        m_left = jnp.where(first_lane, column(from_left, at + cols // 2), pltpu.roll(mask, 1, 1))
        m_right = jnp.where(last_lane, column(from_right, at), pltpu.roll(mask, cols - 1, 1))
        halo_fy = row_recv[0, z:z + 1, :]
        halo_m = row_recv[0, levels + z:levels + z + 1, :]
        fy_up = jnp.where(row32 == 0, jnp.where(is_low, 0.0, halo_fy), pltpu.roll(flux_y, 1, 0))
        m_up = jnp.where(row32 == 0, jnp.where(is_low, 0.0, halo_m), pltpu.roll(mask, 1, 0))
        m_down = jnp.where(
            row32 == rows - 1, jnp.where(is_low, halo_m, 0.0), pltpu.roll(mask, rows - 1, 0))
        diag = ka_ref[z] + flux_x + fx_left + flux_y + fy_up + flux_z + above
        scaled = mask * diag + (1.0 - mask)
        dg[z] = scaled
        prec[z] = 1.0 / (scaled * scaled + ops[z])
        cx[z] = flux_x * mask * m_right
        cxl[z] = fx_left * mask * m_left
        cy[z] = flux_y * mask * m_down
        cyu[z] = fy_up * mask * m_up
        if z + 1 < levels:
            cz[z] = flux_z * mask * wm_ref[z + 1].astype(F32)
        above = flux_z

    def base(k, z):
        return (k * levels + z) * high

    group_lane = lax.broadcasted_iota(jnp.int32, (per_level, 8, cols), 2) - lax.broadcasted_iota(
        jnp.int32, (per_level, 8, cols), 0)

    class Packer:
        def __init__(self):
            self.acc = [[jnp.zeros((8, cols), F32)] * 2 for _ in range(2)]

        def add(self, z, values):
            half, at = z // per_vreg, (z % per_vreg) * per_level
            tiles = jnp.stack(values).reshape(per_level, 8, cols)
            here = group_lane == at
            for side, lane in ((0, cols - 1), (1, 0)):
                edge_col = jnp.broadcast_to(tiles[:, :, lane:lane + 1], tiles.shape)
                self.acc[side][half] = self.acc[side][half] + jnp.sum(
                    jnp.where(here, edge_col, 0.0), axis=0)

        def send(self, slot, field):
            for side in range(2):
                for half in range(2):
                    col_send[slot, side, half] = self.acc[side][half]
            low = field[pl.ds(PAD, samples * levels, stride=high), :]
            top = field[pl.ds(PAD + rows - 1, samples * levels, stride=high), :]
            row_send[slot] = jnp.where(is_low, top, low)
            return exchange(slot)

    def put_rows(slot, field):
        got = row_recv[slot]
        field[pl.ds(PAD - 1, samples * levels, stride=high), :] = jnp.where(is_low, 0.0, got)
        field[pl.ds(PAD + rows, samples * levels, stride=high), :] = jnp.where(is_low, got, 0.0)

    def apply(slot, field, k, z, packs):
        at = base(k, z) + PAD
        here = field[pl.ds(at, rows), :]
        up = field[pl.ds(at - 1, rows), :]
        down = field[pl.ds(at + 1, rows), :]
        half, lane = z // per_vreg, (z % per_vreg) * per_level + k * blocks
        west = jnp.where(first_lane, column(packs[0][half], lane), pltpu.roll(here, 1, 1))
        east = jnp.where(last_lane, column(packs[1][half], lane), pltpu.roll(here, cols - 1, 1))
        total = dg[z] * here - cx[z] * east - cxl[z] * west - cy[z] * down - cyu[z] * up
        if z > 0:
            total = total - cz[z - 1] * field[pl.ds(at - high, rows), :]
        if z + 1 < levels:
            total = total - cz[z] * field[pl.ds(at + high, rows), :]
        return here, total

    def received(slot):
        return [[col_recv[slot, side, half] for half in range(2)] for side in range(2)]

    def fold(value):
        return jnp.sum(value.reshape(blocks, 8, cols), axis=0)

    def store_parts(which, sums):
        for at, value in enumerate(sums):
            part[which, at:at + 1, :] = jnp.sum(value, axis=0, keepdims=True)

    zero = jnp.zeros((8, cols), F32)

    packer = Packer()
    sums = [zero] * (2 * samples)
    for z in range(levels):
        values = []
        for k in range(samples):
            b = bs[k, z]
            p = prec[z] * b
            fa[pl.ds(base(k, z) + PAD, rows), :] = p
            sums[k] = sums[k] + fold(p * b)
            values.append(p)
        packer.add(z, values)
    copies = packer.send(1, fa)
    for copy in copies:
        copy.wait()
    put_rows(1, fa)

    packs = received(1)
    packer = Packer()
    for z in range(levels):
        values = []
        for k in range(samples):
            p, u = apply(1, fa, k, z, packs)
            fb[pl.ds(base(k, z) + PAD, rows), :] = u
            sums[samples + k] = sums[samples + k] + fold(u * u + ops[z] * p * p)
            values.append(u)
        packer.add(z, values)
    store_parts(0, sums)
    copies = packer.send(2, fb)
    red = reduce_start(0)
    for copy in copies:
        copy.wait()
    put_rows(2, fb)

    packs = received(2)
    packer = Packer()
    for z in range(levels):
        values = []
        for k in range(samples):
            _, q = apply(2, fb, k, z, packs)
            q = q + ops[z] * fa[pl.ds(base(k, z) + PAD, rows), :]
            w = prec[z] * q
            out_ref[k, z] = q
            ww[pl.ds(base(k, z) + PAD, rows), :] = w
            values.append(w)
        packer.add(z, values)
    copies = packer.send(3, ww)
    reduce_finish(0, red)
    gamma = [tot[0, k:k + 1, :] for k in range(samples)]
    den = [tot[0, samples + k:samples + k + 1, :] for k in range(samples)]
    alpha = [g / d for g, d in zip(gamma, den)]
    sums = [zero] * (2 * samples)
    for z in range(levels):
        for k in range(samples):
            r = bs[k, z] - alpha[k] * out_ref[k, z]
            zv = prec[z] * r
            sums[k] = sums[k] + fold(zv * r)
            fb[pl.ds(base(k, z) + PAD, rows), :] = zv
    for copy in copies:
        copy.wait()

    got = row_recv[3]
    span = samples * levels
    sample_of = lax.broadcasted_iota(jnp.int32, (span, cols), 0) // levels
    alpha_rows = jnp.zeros((span, cols), F32)
    for k in range(samples):
        alpha_rows = jnp.where(sample_of == k, alpha[k], alpha_rows)
    halo = row_recv[1] - alpha_rows * got
    fb[pl.ds(PAD - 1, span, stride=high), :] = jnp.where(is_low, 0.0, halo)
    fb[pl.ds(PAD + rows, span, stride=high), :] = jnp.where(is_low, halo, 0.0)
    lane_sample = lax.rem(lane1, per_level) // blocks
    alpha_lanes = jnp.zeros((8, cols), F32)
    for k in range(samples):
        alpha_lanes = jnp.where(lane_sample == k, alpha[k], alpha_lanes)
    packs = [
        [a - alpha_lanes * b for a, b in zip(first, second)]
        for first, second in zip(received(1), received(3))
    ]
    for z in range(levels):
        for k in range(samples):
            zv, u = apply(3, fb, k, z, packs)
            sums[samples + k] = sums[samples + k] + fold(u * u + ops[z] * zv * zv)
    store_parts(1, sums)
    red = reduce_start(1)
    reduce_finish(1, red)
    for k in range(samples):
        new = tot[1, k:k + 1, :]
        beta = new / gamma[k]
        step = new / (tot[1, samples + k:samples + k + 1, :] - beta * beta * den[k])
        p_scale = alpha[k] + step * beta
        for z in range(levels):
            at = pl.ds(base(k, z) + PAD, rows)
            out_ref[k, z] = p_scale * fa[at, :] + step * fb[at, :]


def per_device(n_lon, rs, ka, fx, fy, fz, wm, oc, ow, od):
    samples, levels, rows, cols = rs.shape
    count = oc.shape[-1]
    cell = (levels, rows, cols)
    high = rows + 2 * PAD
    field = pltpu.VMEM((samples * levels * high, cols), F32)
    group = 2 * n_lon
    coef = pltpu.VMEM(cell, F32)
    vmem = pl.BlockSpec(memory_space=pltpu.VMEM)
    hbm = pl.BlockSpec(memory_space=pltpu.HBM)
    args = (rs, ka, fx, fy, fz, wm, oc, ow, od)
    return pl.pallas_call(
        functools.partial(kernel, n_lon),
        out_shape=jax.ShapeDtypeStruct(rs.shape, F32),
        in_specs=[hbm] * len(args),
        out_specs=vmem,
        scratch_shapes=[pltpu.VMEM(a.shape, a.dtype) for a in args] + [
            pltpu.VMEM((levels * rows, count), jnp.bfloat16),
            pltpu.VMEM(rs.shape, F32),
            coef, coef, coef, coef, coef, coef, coef, coef,
            field, field, field,
            pltpu.VMEM((4, 2, 2, 8, cols), F32),
            pltpu.VMEM((4, 2, 2, 8, cols), F32),
            pltpu.VMEM((4, samples * levels, cols), F32),
            pltpu.VMEM((4, samples * levels, cols), F32),
            pltpu.VMEM((2, 2 * samples, cols), F32),
            pltpu.VMEM((2, group - 1, 2 * samples, cols), F32),
            pltpu.VMEM((2, 2 * samples, cols), F32),
            pltpu.SemaphoreType.DMA((4, 3)),
            pltpu.SemaphoreType.DMA((4, 3)),
            pltpu.SemaphoreType.DMA((2, group - 1)),
            pltpu.SemaphoreType.DMA((2, group - 1)),
            pltpu.SemaphoreType.DMA((len(args),)),
        ],
        compiler_params=pltpu.CompilerParams(
            collective_id=0, has_side_effects=True, vmem_limit_bytes=60 * 1024 * 1024),
        cost_estimate=pl.CostEstimate(
            flops=4 * 10**9, bytes_accessed=3 * 10**6, transcendentals=0),
    )(*args)


def solution(mesh):
    assert mesh.shape["lat"] == 2
    return jax.shard_map(
        functools.partial(per_device, mesh.shape["lon"]),
        mesh=mesh,
        in_specs=(
            P("grp", None, "lat", "lon"),
            P(None, "lat", "lon"),
            P(None, "lat", "lon"),
            P(None, "lat", "lon"),
            P(None, "lat", "lon"),
            P(None, "lat", "lon"),
            P("lat", "lon", None),
            P("lat", "lon", None),
            P("grp", "lat", "lon", None),
        ),
        out_specs=P("grp", None, "lat", "lon"),
        check_vma=False,
    )
```

```python
import functools

import jax
import jax.numpy as jnp
from jax import lax
from jax.experimental import pallas as pl
from jax.experimental.pallas import tpu as pltpu
from jax.sharding import PartitionSpec as P

MESH = pl.DeviceIdType.MESH
PAD = 8
F32 = jnp.float32


def kernel(
    n_lon, rs_in, ka_in, fx_in, fy_in, fz_in, wm_in, oc_in, ow_in, od_in, out,
    rs_ref, ka_ref, fx_ref, fy_ref, fz_ref, wm_ref, oc_ref, ow_ref, od_ref,
    out_ref, row_hot, bs, ops, prec, dg, cx, cxl, cy, cyu, cz, fa, fb, ww,
    col_send, col_recv, row_send, row_recv, part, slots, tot,
    send_sem, recv_sem, red_send, red_recv, load_sem, out_sem,
):
    samples, levels, rows, cols = rs_ref.shape
    blocks = rows // 8
    high = rows + 2 * PAD
    per_level = samples * blocks
    per_vreg = cols // per_level
    grp, lon, lat = lax.axis_index("grp"), lax.axis_index("lon"), lax.axis_index("lat")
    right = lax.rem(lon + 1, n_lon)
    left = lax.rem(lon + n_lon - 1, n_lon)
    group = 2 * n_lon
    me = lon * 2 + lat

    def peer(step):
        other = lax.rem(me + step, group)
        return (grp, other // 2, lax.rem(other, 2))

    pairs = (
        (wm_in, wm_ref), (fx_in, fx_ref), (fy_in, fy_ref), (oc_in, oc_ref), (ow_in, ow_ref),
        (od_in, od_ref), (rs_in, rs_ref), (ka_in, ka_ref), (fz_in, fz_ref))
    loads = [
        pltpu.make_async_copy(source, here, load_sem.at[at])
        for at, (source, here) in enumerate(pairs)]
    for load in loads:
        load.start()
    barrier = pltpu.get_barrier_semaphore()
    for step in range(1, group):
        pl.semaphore_signal(barrier, inc=1, device_id=peer(step), device_id_type=MESH)

    is_low = lat == 0
    lane1 = lax.broadcasted_iota(jnp.int32, (8, cols), 1)
    lane32 = lax.broadcasted_iota(jnp.int32, (rows, cols), 1)
    row32 = lax.broadcasted_iota(jnp.int32, (rows, cols), 0)
    first_lane, last_lane = lane32 == 0, lane32 == cols - 1

    def exchange(slot):
        copies = []
        for side, target in ((0, (grp, right, lat)), (1, (grp, left, lat))):
            copies.append(pltpu.make_async_remote_copy(
                src_ref=col_send.at[slot, side], dst_ref=col_recv.at[slot, side],
                send_sem=send_sem.at[slot, side], recv_sem=recv_sem.at[slot, side],
                device_id=target, device_id_type=MESH))
        copies.append(pltpu.make_async_remote_copy(
            src_ref=row_send.at[slot], dst_ref=row_recv.at[slot],
            send_sem=send_sem.at[slot, 2], recv_sem=recv_sem.at[slot, 2],
            device_id=(grp, lon, 1 - lat), device_id_type=MESH))
        for copy in (copies[2], copies[0], copies[1]):
            copy.start()
        return copies

    def reduce_start(which):
        copies = []
        for step in range(1, group):
            copies.append(pltpu.make_async_remote_copy(
                src_ref=part.at[which], dst_ref=slots.at[which, step - 1],
                send_sem=red_send.at[which, step - 1], recv_sem=red_recv.at[which, step - 1],
                device_id=peer(step), device_id_type=MESH))
        for copy in copies:
            copy.start()
        return copies

    def reduce_finish(which, copies):
        total = part[which]
        for step, copy in enumerate(copies):
            copy.wait()
            total = total + slots[which, step]
        tot[which] = jnp.broadcast_to(jnp.sum(total, axis=1, keepdims=True), total.shape)

    for load in loads[:3]:
        load.wait()

    to_right = jnp.zeros((8, cols), F32)
    to_left = jnp.zeros((8, cols), F32)
    for z in range(levels):
        for y in range(blocks):
            at = z * blocks + y
            here = pl.ds(y * 8, 8)
            flux = fx_ref[z, here, :]
            mask = wm_ref[z, here, :].astype(F32)
            to_right = jnp.where(lane1 == at, flux[:, cols - 1:cols], to_right)
            to_right = jnp.where(lane1 == at + cols // 2, mask[:, cols - 1:cols], to_right)
            to_left = jnp.where(lane1 == at, mask[:, 0:1], to_left)
    col_send[0, 0, 0] = to_right
    col_send[0, 1, 0] = to_left
    col_send[0, 0, 1] = jnp.zeros((8, cols), F32)
    col_send[0, 1, 1] = jnp.zeros((8, cols), F32)
    row_send[0] = jnp.zeros(row_send.shape[1:], F32)
    for z in range(levels):
        row_send[0, z:z + 1, :] = jnp.where(is_low, fy_ref[z, rows - 1:rows, :], fy_ref[z, 0:1, :])
        row_send[0, levels + z:levels + z + 1, :] = jnp.where(
            is_low, wm_ref[z, rows - 1:rows, :], wm_ref[z, 0:1, :]).astype(F32)

    pl.semaphore_wait(barrier, group - 1)
    copies = exchange(0)

    for load in loads[3:]:
        load.wait()

    count = oc_ref.shape[-1]
    cells = oc_ref[0]
    flat_rows = levels * rows
    hot = lax.broadcasted_iota(jnp.int32, (flat_rows, count), 0) == cells // cols
    row_hot[...] = jnp.where(hot, 1.0, 0.0).astype(jnp.bfloat16)
    lane_hot = lax.broadcasted_iota(jnp.int32, (cols, count), 0) == lax.rem(cells, cols)
    weight = ow_ref[0]

    def scatter(value):
        top = value.astype(jnp.bfloat16).astype(F32)
        low = value - top
        both = jnp.concatenate(
            [jnp.where(lane_hot, top, 0.0), jnp.where(lane_hot, low, 0.0)], axis=0
        ).astype(jnp.bfloat16)
        got = lax.dot_general(
            row_hot[...], both, (((1,), (1,)), ((), ())), preferred_element_type=F32)
        return (got[:, :cols] + got[:, cols:]).reshape(levels, rows, cols)

    ops[...] = scatter(weight)
    for k in range(samples):
        bs[k] = rs_ref[k] + scatter(weight * od_ref[k, 0])

    for copy in copies:
        copy.wait()

    from_left, from_right = col_recv[0, 0, 0], col_recv[0, 1, 0]

    def column(packed, at):
        return jnp.concatenate(
            [jnp.broadcast_to(packed[:, at + y:at + y + 1], (8, cols)) for y in range(blocks)],
            axis=0)

    above = jnp.zeros((rows, cols), F32)
    for z in range(levels):
        mask = wm_ref[z].astype(F32)
        flux_x, flux_y, flux_z = fx_ref[z], fy_ref[z], fz_ref[z]
        at = z * blocks
        fx_left = jnp.where(first_lane, column(from_left, at), pltpu.roll(flux_x, 1, 1))
        m_left = jnp.where(first_lane, column(from_left, at + cols // 2), pltpu.roll(mask, 1, 1))
        m_right = jnp.where(last_lane, column(from_right, at), pltpu.roll(mask, cols - 1, 1))
        halo_fy = row_recv[0, z:z + 1, :]
        halo_m = row_recv[0, levels + z:levels + z + 1, :]
        fy_up = jnp.where(row32 == 0, jnp.where(is_low, 0.0, halo_fy), pltpu.roll(flux_y, 1, 0))
        m_up = jnp.where(row32 == 0, jnp.where(is_low, 0.0, halo_m), pltpu.roll(mask, 1, 0))
        m_down = jnp.where(
            row32 == rows - 1, jnp.where(is_low, halo_m, 0.0), pltpu.roll(mask, rows - 1, 0))
        diag = ka_ref[z] + flux_x + fx_left + flux_y + fy_up + flux_z + above
        scaled = mask * diag + (1.0 - mask)
        dg[z] = scaled
        prec[z] = 1.0 / (scaled * scaled + ops[z])
        cx[z] = flux_x * mask * m_right
        cxl[z] = fx_left * mask * m_left
        cy[z] = flux_y * mask * m_down
        cyu[z] = fy_up * mask * m_up
        if z + 1 < levels:
            cz[z] = flux_z * mask * wm_ref[z + 1].astype(F32)
        above = flux_z

    def base(k, z):
        return (k * levels + z) * high

    group_lane = lax.broadcasted_iota(jnp.int32, (per_level, 8, cols), 2) - lax.broadcasted_iota(
        jnp.int32, (per_level, 8, cols), 0)

    class Packer:
        def __init__(self):
            self.acc = [[jnp.zeros((8, cols), F32)] * 2 for _ in range(2)]

        def add(self, z, values):
            half, at = z // per_vreg, (z % per_vreg) * per_level
            tiles = jnp.stack(values).reshape(per_level, 8, cols)
            here = group_lane == at
            for side, lane in ((0, cols - 1), (1, 0)):
                edge_col = jnp.broadcast_to(tiles[:, :, lane:lane + 1], tiles.shape)
                self.acc[side][half] = self.acc[side][half] + jnp.sum(
                    jnp.where(here, edge_col, 0.0), axis=0)

        def send(self, slot, field):
            for side in range(2):
                for half in range(2):
                    col_send[slot, side, half] = self.acc[side][half]
            low = field[pl.ds(PAD, samples * levels, stride=high), :]
            top = field[pl.ds(PAD + rows - 1, samples * levels, stride=high), :]
            row_send[slot] = jnp.where(is_low, top, low)
            return exchange(slot)

    def put_rows(slot, field):
        got = row_recv[slot]
        field[pl.ds(PAD - 1, samples * levels, stride=high), :] = jnp.where(is_low, 0.0, got)
        field[pl.ds(PAD + rows, samples * levels, stride=high), :] = jnp.where(is_low, got, 0.0)

    def apply(slot, field, k, z, packs):
        at = base(k, z) + PAD
        here = field[pl.ds(at, rows), :]
        up = field[pl.ds(at - 1, rows), :]
        down = field[pl.ds(at + 1, rows), :]
        half, lane = z // per_vreg, (z % per_vreg) * per_level + k * blocks
        west = jnp.where(first_lane, column(packs[0][half], lane), pltpu.roll(here, 1, 1))
        east = jnp.where(last_lane, column(packs[1][half], lane), pltpu.roll(here, cols - 1, 1))
        total = dg[z] * here - cx[z] * east - cxl[z] * west - cy[z] * down - cyu[z] * up
        if z > 0:
            total = total - cz[z - 1] * field[pl.ds(at - high, rows), :]
        if z + 1 < levels:
            total = total - cz[z] * field[pl.ds(at + high, rows), :]
        return here, total

    def received(slot):
        return [[col_recv[slot, side, half] for half in range(2)] for side in range(2)]

    def fold(value):
        return jnp.sum(value.reshape(blocks, 8, cols), axis=0)

    def store_parts(which, sums):
        for at, value in enumerate(sums):
            part[which, at:at + 1, :] = jnp.sum(value, axis=0, keepdims=True)

    zero = jnp.zeros((8, cols), F32)

    packer = Packer()
    sums = [zero] * (2 * samples)
    for z in range(levels):
        values = []
        for k in range(samples):
            b = bs[k, z]
            p = prec[z] * b
            fa[pl.ds(base(k, z) + PAD, rows), :] = p
            sums[k] = sums[k] + fold(p * b)
            values.append(p)
        packer.add(z, values)
    copies = packer.send(1, fa)
    for copy in copies:
        copy.wait()
    put_rows(1, fa)

    packs = received(1)
    packer = Packer()
    for z in range(levels):
        values = []
        for k in range(samples):
            p, u = apply(1, fa, k, z, packs)
            fb[pl.ds(base(k, z) + PAD, rows), :] = u
            sums[samples + k] = sums[samples + k] + fold(u * u + ops[z] * p * p)
            values.append(u)
        packer.add(z, values)
    copies = packer.send(2, fb)
    store_parts(0, sums)
    red = reduce_start(0)
    for copy in copies:
        copy.wait()
    put_rows(2, fb)

    packs = received(2)
    packer = Packer()
    for z in range(levels):
        values = []
        for k in range(samples):
            _, q = apply(2, fb, k, z, packs)
            q = q + ops[z] * fa[pl.ds(base(k, z) + PAD, rows), :]
            w = prec[z] * q
            out_ref[k, z] = q
            ww[pl.ds(base(k, z) + PAD, rows), :] = w
            values.append(w)
        packer.add(z, values)
    copies = packer.send(3, ww)
    reduce_finish(0, red)
    gamma = [tot[0, k:k + 1, :] for k in range(samples)]
    den = [tot[0, samples + k:samples + k + 1, :] for k in range(samples)]
    alpha = [g / d for g, d in zip(gamma, den)]
    sums = [zero] * (2 * samples)
    for z in range(levels):
        for k in range(samples):
            r = bs[k, z] - alpha[k] * out_ref[k, z]
            zv = prec[z] * r
            sums[k] = sums[k] + fold(zv * r)
            fb[pl.ds(base(k, z) + PAD, rows), :] = zv
    for copy in copies:
        copy.wait()

    got = row_recv[3]
    span = samples * levels
    sample_of = lax.broadcasted_iota(jnp.int32, (span, cols), 0) // levels
    alpha_rows = jnp.zeros((span, cols), F32)
    for k in range(samples):
        alpha_rows = jnp.where(sample_of == k, alpha[k], alpha_rows)
    halo = row_recv[1] - alpha_rows * got
    fb[pl.ds(PAD - 1, span, stride=high), :] = jnp.where(is_low, 0.0, halo)
    fb[pl.ds(PAD + rows, span, stride=high), :] = jnp.where(is_low, halo, 0.0)
    lane_sample = lax.rem(lane1, per_level) // blocks
    alpha_lanes = jnp.zeros((8, cols), F32)
    for k in range(samples):
        alpha_lanes = jnp.where(lane_sample == k, alpha[k], alpha_lanes)
    packs = [
        [a - alpha_lanes * b for a, b in zip(first, second)]
        for first, second in zip(received(1), received(3))
    ]
    for z in range(levels):
        for k in range(samples):
            zv, u = apply(3, fb, k, z, packs)
            sums[samples + k] = sums[samples + k] + fold(u * u + ops[z] * zv * zv)
    store_parts(1, sums)
    red = reduce_start(1)
    reduce_finish(1, red)
    stores = [
        pltpu.make_async_copy(out_ref.at[k], out.at[k], out_sem.at[k]) for k in range(samples)]
    for k in range(samples):
        new = tot[1, k:k + 1, :]
        beta = new / gamma[k]
        step = new / (tot[1, samples + k:samples + k + 1, :] - beta * beta * den[k])
        p_scale = alpha[k] + step * beta
        for z in range(levels):
            at = pl.ds(base(k, z) + PAD, rows)
            out_ref[k, z] = p_scale * fa[at, :] + step * fb[at, :]
        stores[k].start()
    for store in stores:
        store.wait()


def per_device(n_lon, rs, ka, fx, fy, fz, wm, oc, ow, od):
    samples, levels, rows, cols = rs.shape
    count = oc.shape[-1]
    cell = (levels, rows, cols)
    high = rows + 2 * PAD
    field = pltpu.VMEM((samples * levels * high, cols), F32)
    group = 2 * n_lon
    coef = pltpu.VMEM(cell, F32)
    hbm = pl.BlockSpec(memory_space=pltpu.HBM)
    args = (rs, ka, fx, fy, fz, wm, oc, ow, od)
    return pl.pallas_call(
        functools.partial(kernel, n_lon),
        out_shape=jax.ShapeDtypeStruct(rs.shape, F32),
        in_specs=[hbm] * len(args),
        out_specs=hbm,
        scratch_shapes=[pltpu.VMEM(a.shape, a.dtype) for a in args] + [
            pltpu.VMEM(rs.shape, F32),
            pltpu.VMEM((levels * rows, count), jnp.bfloat16),
            pltpu.VMEM(rs.shape, F32),
            coef, coef, coef, coef, coef, coef, coef, coef,
            field, field, field,
            pltpu.VMEM((4, 2, 2, 8, cols), F32),
            pltpu.VMEM((4, 2, 2, 8, cols), F32),
            pltpu.VMEM((4, samples * levels, cols), F32),
            pltpu.VMEM((4, samples * levels, cols), F32),
            pltpu.VMEM((2, 2 * samples, cols), F32),
            pltpu.VMEM((2, group - 1, 2 * samples, cols), F32),
            pltpu.VMEM((2, 2 * samples, cols), F32),
            pltpu.SemaphoreType.DMA((4, 3)),
            pltpu.SemaphoreType.DMA((4, 3)),
            pltpu.SemaphoreType.DMA((2, group - 1)),
            pltpu.SemaphoreType.DMA((2, group - 1)),
            pltpu.SemaphoreType.DMA((len(args),)),
            pltpu.SemaphoreType.DMA((samples,)),
        ],
        compiler_params=pltpu.CompilerParams(
            collective_id=0, has_side_effects=True, vmem_limit_bytes=60 * 1024 * 1024),
        cost_estimate=pl.CostEstimate(
            flops=4 * 10**9, bytes_accessed=3 * 10**6, transcendentals=0),
    )(*args)


def solution(mesh):
    assert mesh.shape["lat"] == 2
    return jax.shard_map(
        functools.partial(per_device, mesh.shape["lon"]),
        mesh=mesh,
        in_specs=(
            P("grp", None, "lat", "lon"),
            P(None, "lat", "lon"),
            P(None, "lat", "lon"),
            P(None, "lat", "lon"),
            P(None, "lat", "lon"),
            P(None, "lat", "lon"),
            P("lat", "lon", None),
            P("lat", "lon", None),
            P("grp", "lat", "lon", None),
        ),
        out_specs=P("grp", None, "lat", "lon"),
        check_vma=False,
    )
```

```python
import functools

import jax
import jax.numpy as jnp
from jax import lax
from jax.experimental import pallas as pl
from jax.experimental.pallas import tpu as pltpu
from jax.sharding import PartitionSpec as P

MESH = pl.DeviceIdType.MESH
PAD = 8
F32 = jnp.float32


def kernel(
    n_lon, rs_in, ka_in, fx_in, fy_in, fz_in, wm_in, oc_in, ow_in, od_in, out,
    rs_ref, ka_ref, fx_ref, fy_ref, fz_ref, wm_ref, oc_ref, ow_ref, od_ref,
    out_ref, row_hot, bs, ops, prec, dg, cx, cxl, cy, cyu, cz, ce, fa, fb, ww,
    col_send, col_recv, row_send, row_recv, part, slots, tot,
    send_sem, recv_sem, red_send, red_recv, load_sem, out_sem,
):
    samples, levels, rows, cols = rs_ref.shape
    blocks = rows // 8
    high = rows + 2 * PAD
    per_level = samples * blocks
    per_vreg = cols // per_level
    grp, lon, lat = lax.axis_index("grp"), lax.axis_index("lon"), lax.axis_index("lat")
    right = lax.rem(lon + 1, n_lon)
    left = lax.rem(lon + n_lon - 1, n_lon)
    group = 2 * n_lon
    me = lon * 2 + lat

    def peer(step):
        other = lax.rem(me + step, group)
        return (grp, other // 2, lax.rem(other, 2))

    pairs = (
        (wm_in, wm_ref), (fx_in, fx_ref), (fy_in, fy_ref), (oc_in, oc_ref), (ow_in, ow_ref),
        (od_in, od_ref), (rs_in, rs_ref), (ka_in, ka_ref), (fz_in, fz_ref))
    loads = [
        pltpu.make_async_copy(source, here, load_sem.at[at])
        for at, (source, here) in enumerate(pairs)]
    for load in loads:
        load.start()
    barrier = pltpu.get_barrier_semaphore()
    for step in range(1, group):
        pl.semaphore_signal(barrier, inc=1, device_id=peer(step), device_id_type=MESH)

    is_low = lat == 0
    lane1 = lax.broadcasted_iota(jnp.int32, (8, cols), 1)
    lane32 = lax.broadcasted_iota(jnp.int32, (rows, cols), 1)
    row32 = lax.broadcasted_iota(jnp.int32, (rows, cols), 0)
    first_lane, last_lane = lane32 == 0, lane32 == cols - 1

    def exchange(slot):
        copies = []
        for side, target in ((0, (grp, right, lat)), (1, (grp, left, lat))):
            copies.append(pltpu.make_async_remote_copy(
                src_ref=col_send.at[slot, side], dst_ref=col_recv.at[slot, side],
                send_sem=send_sem.at[slot, side], recv_sem=recv_sem.at[slot, side],
                device_id=target, device_id_type=MESH))
        copies.append(pltpu.make_async_remote_copy(
            src_ref=row_send.at[slot], dst_ref=row_recv.at[slot],
            send_sem=send_sem.at[slot, 2], recv_sem=recv_sem.at[slot, 2],
            device_id=(grp, lon, 1 - lat), device_id_type=MESH))
        for copy in (copies[2], copies[0], copies[1]):
            copy.start()
        return copies

    def reduce_start(which):
        copies = []
        for step in range(1, group):
            copies.append(pltpu.make_async_remote_copy(
                src_ref=part.at[which], dst_ref=slots.at[which, step - 1],
                send_sem=red_send.at[which, step - 1], recv_sem=red_recv.at[which, step - 1],
                device_id=peer(step), device_id_type=MESH))
        for copy in copies:
            copy.start()
        return copies

    def reduce_finish(which, copies):
        total = part[which]
        for step, copy in enumerate(copies):
            copy.wait()
            total = total + slots[which, step]
        tot[which] = jnp.broadcast_to(jnp.sum(total, axis=1, keepdims=True), total.shape)

    for load in loads[:3]:
        load.wait()

    to_right = jnp.zeros((8, cols), F32)
    to_left = jnp.zeros((8, cols), F32)
    for z in range(levels):
        for y in range(blocks):
            at = z * blocks + y
            here = pl.ds(y * 8, 8)
            flux = fx_ref[z, here, :]
            mask = wm_ref[z, here, :].astype(F32)
            to_right = jnp.where(lane1 == at, flux[:, cols - 1:cols], to_right)
            to_right = jnp.where(lane1 == at + cols // 2, mask[:, cols - 1:cols], to_right)
            to_left = jnp.where(lane1 == at, mask[:, 0:1], to_left)
    col_send[0, 0, 0] = to_right
    col_send[0, 1, 0] = to_left
    col_send[0, 0, 1] = jnp.zeros((8, cols), F32)
    col_send[0, 1, 1] = jnp.zeros((8, cols), F32)
    row_send[0] = jnp.zeros(row_send.shape[1:], F32)
    for z in range(levels):
        row_send[0, z:z + 1, :] = jnp.where(is_low, fy_ref[z, rows - 1:rows, :], fy_ref[z, 0:1, :])
        row_send[0, levels + z:levels + z + 1, :] = jnp.where(
            is_low, wm_ref[z, rows - 1:rows, :], wm_ref[z, 0:1, :]).astype(F32)

    pl.semaphore_wait(barrier, group - 1)
    copies = exchange(0)

    for load in loads[3:]:
        load.wait()

    count = oc_ref.shape[-1]
    cells = oc_ref[0]
    flat_rows = levels * rows
    hot = lax.broadcasted_iota(jnp.int32, (flat_rows, count), 0) == cells // cols
    row_hot[...] = jnp.where(hot, 1.0, 0.0).astype(jnp.bfloat16)
    lane_hot = lax.broadcasted_iota(jnp.int32, (cols, count), 0) == lax.rem(cells, cols)
    weight = ow_ref[0]

    def scatter(value):
        top = value.astype(jnp.bfloat16).astype(F32)
        low = value - top
        both = jnp.concatenate(
            [jnp.where(lane_hot, top, 0.0), jnp.where(lane_hot, low, 0.0)], axis=0
        ).astype(jnp.bfloat16)
        got = lax.dot_general(
            row_hot[...], both, (((1,), (1,)), ((), ())), preferred_element_type=F32)
        return (got[:, :cols] + got[:, cols:]).reshape(levels, rows, cols)

    ops[...] = scatter(weight)
    for k in range(samples):
        bs[k] = rs_ref[k] + scatter(weight * od_ref[k, 0])

    for copy in copies:
        copy.wait()

    from_left, from_right = col_recv[0, 0, 0], col_recv[0, 1, 0]

    def column(packed, at):
        return jnp.concatenate(
            [jnp.broadcast_to(packed[:, at + y:at + y + 1], (8, cols)) for y in range(blocks)],
            axis=0)

    above = jnp.zeros((rows, cols), F32)
    for z in range(levels):
        mask = wm_ref[z].astype(F32)
        flux_x, flux_y, flux_z = fx_ref[z], fy_ref[z], fz_ref[z]
        at = z * blocks
        fx_left = jnp.where(first_lane, column(from_left, at), pltpu.roll(flux_x, 1, 1))
        m_left = jnp.where(first_lane, column(from_left, at + cols // 2), pltpu.roll(mask, 1, 1))
        m_right = jnp.where(last_lane, column(from_right, at), pltpu.roll(mask, cols - 1, 1))
        halo_fy = row_recv[0, z:z + 1, :]
        halo_m = row_recv[0, levels + z:levels + z + 1, :]
        fy_up = jnp.where(row32 == 0, jnp.where(is_low, 0.0, halo_fy), pltpu.roll(flux_y, 1, 0))
        m_up = jnp.where(row32 == 0, jnp.where(is_low, 0.0, halo_m), pltpu.roll(mask, 1, 0))
        m_down = jnp.where(
            row32 == rows - 1, jnp.where(is_low, halo_m, 0.0), pltpu.roll(mask, rows - 1, 0))
        diag = ka_ref[z] + flux_x + fx_left + flux_y + fy_up + flux_z + above
        scaled = mask * diag + (1.0 - mask)
        dg[z] = scaled
        prec[z] = 1.0 / (scaled * scaled + ops[z])
        east = flux_x * mask * m_right
        west = fx_left * mask * m_left
        cx[z] = jnp.where(last_lane, 0.0, east)
        cxl[z] = jnp.where(first_lane, 0.0, west)
        ce[z] = jnp.where(first_lane, west, jnp.where(last_lane, east, 0.0))
        cy[z] = flux_y * mask * m_down
        cyu[z] = fy_up * mask * m_up
        if z + 1 < levels:
            cz[z] = flux_z * mask * wm_ref[z + 1].astype(F32)
        above = flux_z

    def base(k, z):
        return (k * levels + z) * high

    group_lane = lax.broadcasted_iota(jnp.int32, (per_level, 8, cols), 2) - lax.broadcasted_iota(
        jnp.int32, (per_level, 8, cols), 0)

    class Packer:
        def __init__(self):
            self.acc = [[jnp.zeros((8, cols), F32)] * 2 for _ in range(2)]

        def add(self, z, values):
            half, at = z // per_vreg, (z % per_vreg) * per_level
            tiles = jnp.stack(values).reshape(per_level, 8, cols)
            here = group_lane == at
            for side, lane in ((0, cols - 1), (1, 0)):
                edge_col = jnp.broadcast_to(tiles[:, :, lane:lane + 1], tiles.shape)
                self.acc[side][half] = self.acc[side][half] + jnp.sum(
                    jnp.where(here, edge_col, 0.0), axis=0)

        def send(self, slot, field):
            for side in range(2):
                for half in range(2):
                    col_send[slot, side, half] = self.acc[side][half]
            low = field[pl.ds(PAD, samples * levels, stride=high), :]
            top = field[pl.ds(PAD + rows - 1, samples * levels, stride=high), :]
            row_send[slot] = jnp.where(is_low, top, low)
            return exchange(slot)

    def put_rows(slot, field):
        got = row_recv[slot]
        field[pl.ds(PAD - 1, samples * levels, stride=high), :] = jnp.where(is_low, 0.0, got)
        field[pl.ds(PAD + rows, samples * levels, stride=high), :] = jnp.where(is_low, got, 0.0)

    def inside(field, k, z):
        at = base(k, z) + PAD
        here = field[pl.ds(at, rows), :]
        total = dg[z] * here - cx[z] * pltpu.roll(here, cols - 1, 1) - cxl[z] * pltpu.roll(here, 1, 1)
        if z > 0:
            total = total - cz[z - 1] * field[pl.ds(at - high, rows), :]
        if z + 1 < levels:
            total = total - cz[z] * field[pl.ds(at + high, rows), :]
        return total

    def finish(total, field, k, z, packs):
        at = base(k, z) + PAD
        half, lane = z // per_vreg, (z % per_vreg) * per_level + k * blocks
        side = jnp.where(first_lane, column(packs[0][half], lane), column(packs[1][half], lane))
        return (total - cy[z] * field[pl.ds(at + 1, rows), :]
                - cyu[z] * field[pl.ds(at - 1, rows), :] - ce[z] * side)

    def received(slot):
        return [[col_recv[slot, side, half] for half in range(2)] for side in range(2)]

    def fold(value):
        return jnp.sum(value.reshape(blocks, 8, cols), axis=0)

    def store_parts(which, sums):
        for at, value in enumerate(sums):
            part[which, at:at + 1, :] = jnp.sum(value, axis=0, keepdims=True)

    zero = jnp.zeros((8, cols), F32)

    packer = Packer()
    sums = [zero] * (2 * samples)
    for z in range(levels):
        values = []
        for k in range(samples):
            b = bs[k, z]
            p = prec[z] * b
            fa[pl.ds(base(k, z) + PAD, rows), :] = p
            sums[k] = sums[k] + fold(p * b)
            values.append(p)
        packer.add(z, values)
    copies = packer.send(1, fa)
    for z in range(levels):
        for k in range(samples):
            fb[pl.ds(base(k, z) + PAD, rows), :] = inside(fa, k, z)
    for copy in copies:
        copy.wait()
    put_rows(1, fa)

    packs = received(1)
    packer = Packer()
    for z in range(levels):
        values = []
        for k in range(samples):
            at = pl.ds(base(k, z) + PAD, rows)
            p = fa[at, :]
            u = finish(fb[at, :], fa, k, z, packs)
            fb[at, :] = u
            sums[samples + k] = sums[samples + k] + fold(u * u + ops[z] * p * p)
            values.append(u)
        packer.add(z, values)
    copies = packer.send(2, fb)
    store_parts(0, sums)
    red = reduce_start(0)
    for z in range(levels):
        for k in range(samples):
            p = fa[pl.ds(base(k, z) + PAD, rows), :]
            out_ref[k, z] = inside(fb, k, z) + ops[z] * p
    for copy in copies:
        copy.wait()
    put_rows(2, fb)

    packs = received(2)
    packer = Packer()
    for z in range(levels):
        values = []
        for k in range(samples):
            q = finish(out_ref[k, z], fb, k, z, packs)
            w = prec[z] * q
            out_ref[k, z] = q
            ww[pl.ds(base(k, z) + PAD, rows), :] = w
            values.append(w)
        packer.add(z, values)
    copies = packer.send(3, ww)
    reduce_finish(0, red)
    gamma = [tot[0, k:k + 1, :] for k in range(samples)]
    den = [tot[0, samples + k:samples + k + 1, :] for k in range(samples)]
    alpha = [g / d for g, d in zip(gamma, den)]
    sums = [zero] * (2 * samples)
    for z in range(levels):
        for k in range(samples):
            r = bs[k, z] - alpha[k] * out_ref[k, z]
            zv = prec[z] * r
            sums[k] = sums[k] + fold(zv * r)
            fb[pl.ds(base(k, z) + PAD, rows), :] = zv
    for z in range(levels):
        for k in range(samples):
            ww[pl.ds(base(k, z) + PAD, rows), :] = inside(fb, k, z)
    for copy in copies:
        copy.wait()

    got = row_recv[3]
    span = samples * levels
    sample_of = lax.broadcasted_iota(jnp.int32, (span, cols), 0) // levels
    alpha_rows = jnp.zeros((span, cols), F32)
    for k in range(samples):
        alpha_rows = jnp.where(sample_of == k, alpha[k], alpha_rows)
    halo = row_recv[1] - alpha_rows * got
    fb[pl.ds(PAD - 1, span, stride=high), :] = jnp.where(is_low, 0.0, halo)
    fb[pl.ds(PAD + rows, span, stride=high), :] = jnp.where(is_low, halo, 0.0)
    lane_sample = lax.rem(lane1, per_level) // blocks
    alpha_lanes = jnp.zeros((8, cols), F32)
    for k in range(samples):
        alpha_lanes = jnp.where(lane_sample == k, alpha[k], alpha_lanes)
    packs = [
        [a - alpha_lanes * b for a, b in zip(first, second)]
        for first, second in zip(received(1), received(3))
    ]
    for z in range(levels):
        for k in range(samples):
            at = pl.ds(base(k, z) + PAD, rows)
            zv = fb[at, :]
            u = finish(ww[at, :], fb, k, z, packs)
            sums[samples + k] = sums[samples + k] + fold(u * u + ops[z] * zv * zv)
    store_parts(1, sums)
    red = reduce_start(1)
    reduce_finish(1, red)
    stores = [
        pltpu.make_async_copy(out_ref.at[k], out.at[k], out_sem.at[k]) for k in range(samples)]
    for k in range(samples):
        new = tot[1, k:k + 1, :]
        beta = new / gamma[k]
        step = new / (tot[1, samples + k:samples + k + 1, :] - beta * beta * den[k])
        p_scale = alpha[k] + step * beta
        for z in range(levels):
            at = pl.ds(base(k, z) + PAD, rows)
            out_ref[k, z] = p_scale * fa[at, :] + step * fb[at, :]
        stores[k].start()
    for store in stores:
        store.wait()


def per_device(n_lon, rs, ka, fx, fy, fz, wm, oc, ow, od):
    samples, levels, rows, cols = rs.shape
    count = oc.shape[-1]
    cell = (levels, rows, cols)
    high = rows + 2 * PAD
    field = pltpu.VMEM((samples * levels * high, cols), F32)
    group = 2 * n_lon
    coef = pltpu.VMEM(cell, F32)
    hbm = pl.BlockSpec(memory_space=pltpu.HBM)
    args = (rs, ka, fx, fy, fz, wm, oc, ow, od)
    return pl.pallas_call(
        functools.partial(kernel, n_lon),
        out_shape=jax.ShapeDtypeStruct(rs.shape, F32),
        in_specs=[hbm] * len(args),
        out_specs=hbm,
        scratch_shapes=[pltpu.VMEM(a.shape, a.dtype) for a in args] + [
            pltpu.VMEM(rs.shape, F32),
            pltpu.VMEM((levels * rows, count), jnp.bfloat16),
            pltpu.VMEM(rs.shape, F32),
            coef, coef, coef, coef, coef, coef, coef, coef, coef,
            field, field, field,
            pltpu.VMEM((4, 2, 2, 8, cols), F32),
            pltpu.VMEM((4, 2, 2, 8, cols), F32),
            pltpu.VMEM((4, samples * levels, cols), F32),
            pltpu.VMEM((4, samples * levels, cols), F32),
            pltpu.VMEM((2, 2 * samples, cols), F32),
            pltpu.VMEM((2, group - 1, 2 * samples, cols), F32),
            pltpu.VMEM((2, 2 * samples, cols), F32),
            pltpu.SemaphoreType.DMA((4, 3)),
            pltpu.SemaphoreType.DMA((4, 3)),
            pltpu.SemaphoreType.DMA((2, group - 1)),
            pltpu.SemaphoreType.DMA((2, group - 1)),
            pltpu.SemaphoreType.DMA((len(args),)),
            pltpu.SemaphoreType.DMA((samples,)),
        ],
        compiler_params=pltpu.CompilerParams(
            collective_id=0, has_side_effects=True, vmem_limit_bytes=60 * 1024 * 1024),
        cost_estimate=pl.CostEstimate(
            flops=4 * 10**9, bytes_accessed=3 * 10**6, transcendentals=0),
    )(*args)


def solution(mesh):
    assert mesh.shape["lat"] == 2
    return jax.shard_map(
        functools.partial(per_device, mesh.shape["lon"]),
        mesh=mesh,
        in_specs=(
            P("grp", None, "lat", "lon"),
            P(None, "lat", "lon"),
            P(None, "lat", "lon"),
            P(None, "lat", "lon"),
            P(None, "lat", "lon"),
            P(None, "lat", "lon"),
            P("lat", "lon", None),
            P("lat", "lon", None),
            P("grp", "lat", "lon", None),
        ),
        out_specs=P("grp", None, "lat", "lon"),
        check_vma=False,
    )
```
